512 devices in a mesh: rows: 64 (over x, z), mass: 8 (over y, core).
Axes of the slice: x: 4, y: 4, z: 16, core: 2. Of those that a mesh axis runs over, the one named last changes fastest.
Arguments:
- data: bfloat16 [98304, 4096], P('rows', 'mass'), may hold values from -3 to 580
- conc_init: float32 [64, 98304], P(None, 'rows'), may hold values from 0.05 to 3.5, as said below
- spec_init: float32 [64, 4096], P(None, 'mass'), may hold values from 0.05 to 3.5, as said below
Outputs:
- concentrations: float32 [64, 98304], P(None, 'rows')
- spectra: float32 [64, 4096], P(None, 'mass')
The draws below stay inside these ranges and needn't reach their ends.
Inputs may be any that keep to these rules, and one draw needn't show every extreme that they name: `conc_init`: positive. `spec_init`: positive.
All inputs are finite; a program needn't handle non-finite values.
Results may differ from the reference program's by a relative error of at most 0.0017.
The reference program's roundings to bfloat16 on the way (of `spec_low` and `conc_low`) count: a program that leaves them out, or rounds other values in their place, can miss the bound.
Values sent between devices are 32-bit elements; how exact they have to be, the bound alone decides.
No kernel may reach another device: no remote copies, remote signals or barrier semaphores. Data moves between devices by JAX's collectives and lax.ppermute only.
A program may use at most 64 MiB of HBM per device.

```python
import jax
import jax.numpy as jnp
from jax import lax

COMPONENTS = 64
CHANNELS = 4096
ROWS_DEV = 1536
ITERS = 2
PIXELS = 98304


def ramp_levels(length):
    steps = 1 + 3 * jnp.arange(length, dtype=jnp.int32) // length
    return steps.astype(jnp.float32)


def truths(key):
    conc_key = jax.random.fold_in(key, 101)
    spec_key = jax.random.fold_in(key, 202)
    region_key, level_key = jax.random.split(conc_key)
    peak_key, height_key = jax.random.split(spec_key)
    hot_blocks = jax.random.randint(region_key, (COMPONENTS, PIXELS // ROWS_DEV), 0, 4) == 0
    hot_rows = jnp.repeat(hot_blocks, ROWS_DEV, axis=1)
    conc_levels = jax.random.randint(level_key, (COMPONENTS, PIXELS), 0, 16)
    conc_whole = (1 + jnp.where(hot_rows, conc_levels, 0)).astype(jnp.float32)
    conc_true = conc_whole * ramp_levels(PIXELS)[None, :] / 16.0
    hot_peaks = jax.random.randint(peak_key, (COMPONENTS, CHANNELS), 0, 4) == 0
    spec_levels = jax.random.randint(height_key, (COMPONENTS, CHANNELS), 0, 16)
    spec_whole = (1 + jnp.where(hot_peaks, spec_levels, 0)).astype(jnp.float32)
    spec_true = spec_whole * ramp_levels(CHANNELS)[None, :] / 16.0
    return (conc_true, spec_true)


def draw_data(key, part):
    conc_true, spec_true = truths(key)
    key = jax.random.fold_in(key, 5)
    clean = jnp.dot(conc_true.T, spec_true, precision=lax.Precision.HIGHEST)
    noise = jnp.clip(0.5 * jax.random.normal(key, (PIXELS, CHANNELS), jnp.float32), -3.0, 3.0)
    return (clean + noise).astype(jnp.bfloat16)


def draw_conc_init(key, part):
    conc_true, spec_true = truths(key)
    key = jax.random.fold_in(key, 11)
    factor = jax.random.uniform(key, (COMPONENTS, PIXELS), jnp.float32, 0.9, 1.1)
    return conc_true * factor


def draw_spec_init(key, part):
    conc_true, spec_true = truths(key)
    key = jax.random.fold_in(key, 23)
    factor = jax.random.uniform(key, (COMPONENTS, CHANNELS), jnp.float32, 0.9, 1.1)
    return spec_true * factor


def setup_inputs(seed: int = 0) -> dict:
    arg_keys = jax.random.split(jax.random.key(seed), 4)
    return {
        "data": draw_data(jax.random.fold_in(arg_keys[3], 71), 0),
        "conc_init": draw_conc_init(jax.random.fold_in(arg_keys[3], 71), 0),
        "spec_init": draw_spec_init(jax.random.fold_in(arg_keys[3], 71), 0),
    }


def sweep_rows(factor, cross, gram):
    for index in range(COMPONENTS):
        mixed = jnp.dot(gram[index], factor, precision=lax.Precision.HIGHEST)
        updated = factor[index] + (cross[index] - mixed) / gram[index, index]
        factor = factor.at[index].set(jnp.maximum(updated, 1e-4))
    return factor


def reference(data, conc_init, spec_init):
    concentrations = conc_init
    spectra = spec_init
    inner = (((1,), (1,)), ((), ()))
    for step in range(ITERS):
        spec_low = spectra.astype(jnp.bfloat16)
        conc_cross = lax.dot_general(spec_low, data, inner, preferred_element_type=jnp.float32)
        spec_gram = lax.dot_general(spectra, spectra, inner, precision=lax.Precision.HIGHEST)
        concentrations = sweep_rows(concentrations, conc_cross, spec_gram)
        conc_low = concentrations.astype(jnp.bfloat16)
        spec_cross = jnp.dot(conc_low, data, preferred_element_type=jnp.float32)
        conc_gram = lax.dot_general(concentrations, concentrations, inner, precision=lax.Precision.HIGHEST)
        spectra = sweep_rows(spectra, spec_cross, conc_gram)
    return concentrations, spectra
```

```python
import jax
import jax.numpy as jnp
from jax import lax
from jax.experimental import pallas as pl
from jax.experimental.pallas import tpu as pltpu
from jax.sharding import PartitionSpec as P

ITERS = 2
COMPS = 64
FLOOR = 1e-4
NT = (((1,), (1,)), ((), ()))
CHUNK = 512

def holder(x, pair, low):
    return x * 16 + pair * 2 + (low ^ (pair >= 4))


NEAR = [[holder(x, pair, low) for x in range(4) for low in range(2)] for pair in range(8)]
FAR = [[holder(x, pair, low) for pair in range(8)] for x in range(4) for low in range(2)]


def gram_of(factor):
    return lax.dot_general(
        factor, factor, NT, precision=lax.Precision.HIGHEST, preferred_element_type=jnp.float32
    )


def sweep(sums, width, old, new, held):
    gram = sums[:, width : width + COMPS]
    rows = lax.broadcasted_iota(jnp.int32, (COMPS, COMPS), 0)
    cols = lax.broadcasted_iota(jnp.int32, (COMPS, COMPS), 1)
    diag = jnp.sum(jnp.where(rows == cols, gram, 0.0), axis=1, keepdims=True)
    inverse = 1.0 / diag
    scaled = gram * inverse
    upper = jnp.where(cols > rows, scaled, 0.0)
    lower = jnp.where(cols < rows, scaled, 0.0)
    held[...] = sums[:, :width] * inverse - jnp.dot(
        upper, old[...], precision=lax.Precision.HIGHEST, preferred_element_type=jnp.float32
    )
    for block in range(0, COMPS, 8):
        own = held[block : block + 8, :]
        for index in range(7):
            row = jnp.maximum(own[index : index + 1, :], FLOOR)
            own = own - lower[block : block + 8, block + index : block + index + 1] * row
        own = jnp.maximum(own, FLOOR)
        new[block : block + 8, :] = own
        for start in range(0, width, CHUNK):
            part = [own[i : i + 1, start : start + CHUNK] for i in range(8)]
            for later in range(block + 8, COMPS, 8):
                total = held[later : later + 8, start : start + CHUNK]
                for i in range(8):
                    total = total - lower[later : later + 8, block + i : block + i + 1] * part[i]
                held[later : later + 8, start : start + CHUNK] = total


def put_spec_terms(spectra, data, out):
    pixels = data.shape[0]
    out[:, :pixels] = lax.dot_general(
        spectra.astype(jnp.bfloat16), data[...], NT, preferred_element_type=jnp.float32
    )
    out[:, pixels : pixels + COMPS] = gram_of(spectra)
    out[:, pixels + COMPS :] = jnp.zeros_like(out[:, pixels + COMPS :])


def put_conc_terms(conc, data, out):
    channels = data.shape[1]
    out[:, :channels] = jnp.dot(
        conc.astype(jnp.bfloat16), data[...], preferred_element_type=jnp.float32
    )
    out[:, channels : channels + COMPS] = gram_of(conc)
    out[:, channels + COMPS :] = jnp.zeros_like(out[:, channels + COMPS :])


def first_kernel(data, spec, out):
    put_spec_terms(spec[...], data, out)


def conc_kernel(sums, old, data, new, out, held):
    sweep(sums, old.shape[1], old, new, held)
    put_conc_terms(new[...], data, out)


def spec_kernel(sums, old, data, new, out, held):
    sweep(sums, old.shape[1], old, new, held)
    put_spec_terms(new[...], data, out)


def last_kernel(sums, old, new, held):
    sweep(sums, old.shape[1], old, new, held)


def f32(*shape):
    return jax.ShapeDtypeStruct(shape, jnp.float32)


def call(kernel, outs, *args, held=None):
    return pl.pallas_call(
        kernel,
        out_shape=outs,
        scratch_shapes=[] if held is None else [pltpu.VMEM(held, jnp.float32)],
        compiler_params=pltpu.CompilerParams(vmem_limit_bytes=24 << 20),
    )(*args)


def padded(width):
    return -(-(width + COMPS) // 128) * 128


def exchange(parts, axis, groups=None):
    return lax.all_to_all(parts, axis, 0, 0, axis_index_groups=groups)


def to_all(share, axis, groups=None):
    return exchange(jnp.broadcast_to(share, (8,) + share.shape), axis, groups)


def sum_mass(terms):
    parts = exchange(terms.reshape(8, 8, -1), "mass")
    return to_all(jnp.sum(parts, axis=0), "mass").reshape(terms.shape)


def sum_rows(terms):
    parts = exchange(terms.reshape(8, 8, -1), "rows", NEAR)
    parts = to_all(jnp.sum(parts, axis=0), "rows", FAR)
    return to_all(jnp.sum(parts, axis=0), "rows", NEAR).reshape(terms.shape)


def body(data, conc, spec):
    pixels, channels = data.shape
    wide, narrow = f32(COMPS, padded(pixels)), f32(COMPS, padded(channels))
    terms = call(first_kernel, wide, data, spec)
    for step in range(ITERS):
        sums = sum_mass(terms)
        conc, terms = call(
            conc_kernel, (f32(*conc.shape), narrow), sums, conc, data, held=conc.shape
        )
        sums = sum_rows(terms)
        if step < ITERS - 1:
            spec, terms = call(
                spec_kernel, (f32(*spec.shape), wide), sums, spec, data, held=spec.shape
            )
        else:
            spec = call(last_kernel, f32(*spec.shape), sums, spec, held=spec.shape)
    return conc, spec


def solution(mesh):
    return jax.shard_map(
        body,
        mesh=mesh,
        in_specs=(P("rows", "mass"), P(None, "rows"), P(None, "mass")),
        out_specs=(P(None, "rows"), P(None, "mass")),
        check_vma=False,
    )
```

```python
import jax
import jax.numpy as jnp
from jax import lax
from jax.experimental import pallas as pl
from jax.experimental.pallas import tpu as pltpu
from jax.sharding import PartitionSpec as P

ITERS = 2
COMPS = 64
FLOOR = 1e-4
NT = (((1,), (1,)), ((), ()))
LANES = 128
CHUNK = 256


def holder(x, pair, low):
    return x * 16 + pair * 2 + (low ^ (pair >= 4))


NEAR = [[holder(x, pair, low) for x in range(4) for low in range(2)] for pair in range(8)]
FAR = [[holder(x, pair, low) for pair in range(8)] for x in range(4) for low in range(2)]
COLUMN = [[y * 2 + core for y in range(4)] for core in range(2)]
SIBLING = [(i, i ^ 1) for i in range(8)]


def gram_of(factor):
    return lax.dot_general(
        factor, factor, NT, precision=lax.Precision.HIGHEST, preferred_element_type=jnp.float32
    )


def half_rows(index, half):
    return pl.ds(pl.multiple_of(index * half, half), half)


def tiles_of(width):
    return COMPS // 8 * (width // LANES) + COMPS // 16


def put_cross_tiles(out, cross):
    across = cross.shape[1] // LANES
    for i in range(COMPS // 8):
        for j in range(across):
            out[i * across + j] = cross[i * 8 : i * 8 + 8, j * LANES : (j + 1) * LANES]


def put_gram_tiles(out, gram, first):
    for i in range(COMPS // 16):
        out[first + i] = jnp.concatenate(
            [gram[i * 16 : i * 16 + 8, :], gram[i * 16 + 8 : i * 16 + 16, :]], axis=1
        )


def take_tiles(tile, width):
    across = width // LANES
    cross = jnp.concatenate(
        [
            jnp.concatenate([tile(i * across + j) for j in range(across)], axis=1)
            for i in range(COMPS // 8)
        ],
        axis=0,
    )
    first = COMPS // 8 * across
    gram = []
    for i in range(COMPS // 16):
        pair = tile(first + i)
        gram += [pair[:, :COMPS], pair[:, COMPS:]]
    return cross, jnp.concatenate(gram, axis=0)


def pieces_of(width):
    return 2 * (width // LANES) + 1


def put_pieces(out, cross, gram):
    across = cross.shape[1] // LANES
    for share in range(8):
        for low in range(2):
            rows = slice(share * 8 + low * 4, share * 8 + low * 4 + 4)
            for j in range(across):
                out[share, 2 * j + low] = cross[rows, j * LANES : (j + 1) * LANES]
        upper, lower = gram[share * 8 : share * 8 + 4, :], gram[share * 8 + 4 : share * 8 + 8, :]
        out[share, 2 * across] = jnp.concatenate([upper, lower], axis=1)


def take_pieces(pieces, width):
    across = width // LANES
    cross, gram = [], []
    for share in range(8):
        tiles = [
            jnp.concatenate([pieces[share, 2 * j], pieces[share, 2 * j + 1]], axis=0)
            for j in range(across)
        ]
        cross.append(jnp.concatenate(tiles, axis=1))
        both = pieces[share, 2 * across]
        gram += [both[:, :COMPS], both[:, COMPS:]]
    return jnp.concatenate(cross, axis=0), jnp.concatenate(gram, axis=0)


def sweep(cross, gram, old, new, held, done=None):
    width = cross.shape[1]
    rows = lax.broadcasted_iota(jnp.int32, (COMPS, COMPS), 0)
    cols = lax.broadcasted_iota(jnp.int32, (COMPS, COMPS), 1)
    diag = jnp.sum(jnp.where(rows == cols, gram, 0.0), axis=1, keepdims=True)
    inverse = 1.0 / diag
    scaled = gram * inverse
    upper = jnp.where(cols > rows, scaled, 0.0)
    lower = jnp.where(cols < rows, scaled, 0.0)
    held[...] = cross * inverse - jnp.dot(
        upper, old, precision=lax.Precision.HIGHEST, preferred_element_type=jnp.float32
    )
    for block in range(0, COMPS, 8):
        own = held[block : block + 8, :]
        for index in range(7):
            row = jnp.maximum(own[index : index + 1, :], FLOOR)
            own = own - lower[block : block + 8, block + index : block + index + 1] * row
        own = jnp.maximum(own, FLOOR)
        new[block : block + 8, :] = own
        if done is not None:
            done(block // 8)
        for start in range(0, width, CHUNK):
            part = [own[i : i + 1, start : start + CHUNK] for i in range(8)]
            for later in range(block + 8, COMPS, 8):
                total = held[later : later + 8, start : start + CHUNK]
                for i in range(8):
                    total = total - lower[later : later + 8, block + i : block + i + 1] * part[i]
                held[later : later + 8, start : start + CHUNK] = total


def spec_cross(low, data):
    return lax.dot_general(low, data, NT, preferred_element_type=jnp.float32)


def spec_terms(core, spectra, data, out):
    half = data.shape[0] // 2
    cross = spec_cross(spectra.astype(jnp.bfloat16), data[half_rows(core, half), :])
    put_cross_tiles(out, cross)


def first_kernel(core, spec, data, send):
    spec_terms(1 - core[0], spec[...], data, send)
    put_gram_tiles(send, gram_of(spec[...]), send.shape[0] - COMPS // 16)


def spec_kernel(core, sums, old, data, new, send, held):
    cross, gram = take_pieces(sums, old.shape[1])
    sweep(cross, gram, old[...], new, held)
    first_kernel(core, new, data, send)


def keep_kernel(core, spec, data, send, keep):
    spec_terms(core[0], spec[...], data, keep)
    first = keep.shape[0] - COMPS // 16
    keep[first:] = send[first:]


def conc_sweep_kernel(core, parts, old, new, held):
    half = new.shape[1]
    cross, gram = take_tiles(
        lambda i: (parts[0, i] + parts[1, i]) + (parts[2, i] + parts[3, i]), half
    )
    if old.shape[1] == half:
        before = old[...]
    else:
        before = old[:, half_rows(core[0], half)]
    sweep(cross, gram, before, new, held)


def conc_terms(core, part, data):
    half = part.shape[1]
    cross = jnp.dot(
        part.astype(jnp.bfloat16), data[half_rows(core, half), :], preferred_element_type=jnp.float32
    )
    return cross, gram_of(part)


def own_terms_kernel(core, own, data, out):
    channels = data.shape[1]
    cross, gram = conc_terms(core[0], own[...], data)
    out[:, :channels] = cross
    out[:, channels : channels + COMPS] = gram
    out[:, channels + COMPS :] = jnp.zeros_like(out[:, channels + COMPS :])


def all_terms_kernel(core, other, data, own_terms, out):
    channels = data.shape[1]
    cross, gram = conc_terms(1 - core[0], other[...], data)
    put_pieces(
        out,
        own_terms[:, :channels] + cross,
        own_terms[:, channels : channels + COMPS] + gram,
    )


def last_kernel(core, sums, old, own, other, conc, spec, new, held, sems):
    half = own.shape[1]
    copies = [
        pltpu.make_async_copy(part, conc.at[:, half_rows(index, half)], sems.at[i])
        for i, (part, index) in enumerate(((own, core[0]), (other, 1 - core[0])))
    ]
    for copy in copies:
        copy.start()

    def done(block):
        rows = pl.ds(block * 8, 8)
        copies.append(pltpu.make_async_copy(new.at[rows, :], spec.at[rows, :], sems.at[2 + block]))
        copies[-1].start()

    cross, gram = take_pieces(sums, old.shape[1])
    sweep(cross, gram, old[...], new, held, done)
    for copy in copies:
        copy.wait()


def f32(*shape):
    return jax.ShapeDtypeStruct(shape, jnp.float32)


VMEM = pl.BlockSpec(memory_space=pltpu.VMEM)
SMEM = pl.BlockSpec(memory_space=pltpu.SMEM)
HBM = pl.BlockSpec(memory_space=pltpu.HBM)


def call(kernel, outs, specs, scratch, *args, space=VMEM):
    return pl.pallas_call(
        kernel,
        out_shape=outs,
        in_specs=specs,
        out_specs=jax.tree.map(lambda _: space, outs),
        scratch_shapes=scratch,
        compiler_params=pltpu.CompilerParams(vmem_limit_bytes=24 << 20),
        cost_estimate=pl.CostEstimate(
            flops=200_000_000, bytes_accessed=2_000_000, transcendentals=0
        ),
    )(*args)


def exchange(parts, axis, groups):
    return lax.all_to_all(parts, axis, 0, 0, axis_index_groups=groups)


def to_all(share, axis, groups):
    members = len(groups[0])
    return exchange(jnp.broadcast_to(share, (members,) + share.shape), axis, groups)


def swap(half):
    return lax.ppermute(half, "mass", SIBLING)


def sum_rows(terms):
    parts = exchange(terms, "rows", NEAR)
    parts = to_all(jnp.sum(parts, axis=0), "rows", FAR)
    return to_all(jnp.sum(parts, axis=0), "rows", NEAR)


def body(data, conc, spec):
    pixels, channels = data.shape
    half = pixels // 2
    core = lax.rem(lax.axis_index("mass"), 2).reshape(1)
    tiles, narrow = f32(tiles_of(half), 8, LANES), f32(COMPS, channels + LANES)
    pieces = f32(8, pieces_of(channels), 4, LANES)
    held = pltpu.VMEM((COMPS, half), jnp.float32)
    spec_held = pltpu.VMEM(spec.shape, jnp.float32)
    send = call(first_kernel, tiles, [SMEM, VMEM, VMEM], [], core, spec, data)
    own = conc
    for step in range(ITERS):
        arriving = swap(send)
        keep = call(keep_kernel, tiles, [SMEM, VMEM, VMEM, VMEM], [], core, spec, data, send)
        parts = to_all(keep + arriving, "mass", COLUMN)
        own = call(
            conc_sweep_kernel, f32(COMPS, half), [SMEM, VMEM, VMEM], [held], core, parts, own
        )
        other = swap(own)
        terms = call(own_terms_kernel, narrow, [SMEM, VMEM, VMEM], [], core, own, data)
        terms = call(
            all_terms_kernel, pieces, [SMEM, VMEM, VMEM, VMEM], [], core, other, data, terms
        )
        sums = sum_rows(terms)
        if step < ITERS - 1:
            spec, send = call(
                spec_kernel,
                (f32(*spec.shape), tiles),
                [SMEM, VMEM, VMEM, VMEM],
                [spec_held],
                core,
                sums,
                spec,
                data,
            )
        else:
            conc, spec = call(
                last_kernel,
                (f32(*conc.shape), f32(*spec.shape)),
                [SMEM, VMEM, VMEM, VMEM, VMEM],
                [spec_held, spec_held, pltpu.SemaphoreType.DMA((10,))],
                core,
                sums,
                spec,
                own,
                other,
                space=HBM,
            )
    return conc, spec


def solution(mesh):
    return jax.shard_map(
        body,
        mesh=mesh,
        in_specs=(P("rows", "mass"), P(None, "rows"), P(None, "mass")),
        out_specs=(P(None, "rows"), P(None, "mass")),
        check_vma=False,
    )
```

```python
import jax
import jax.numpy as jnp
from jax import lax
from jax.experimental import pallas as pl
from jax.experimental.pallas import tpu as pltpu
from jax.sharding import PartitionSpec as P

ITERS = 2
COMPS = 64
FLOOR = 1e-4
NT = (((1,), (1,)), ((), ()))
LANES = 128
CHUNK = 256


def holder(x, pair, low):
    return x * 16 + pair * 2 + (low ^ (pair >= 4))


MIDDLE = (2, 3, 0, 1)
MIDDLE_PAIRS = (4, 5, 6, 7, 0, 1, 2, 3)
NEAR = [[holder(x, pair, low) for x in MIDDLE for low in range(2)] for pair in range(8)]
FAR = [[holder(x, pair, low) for pair in MIDDLE_PAIRS] for x in range(4) for low in range(2)]
COLUMN = [[y * 2 + core for y in MIDDLE] for core in range(2)]
SIBLING = [(i, i ^ 1) for i in range(8)]


def gram_of(factor):
    return lax.dot_general(
        factor, factor, NT, precision=lax.Precision.HIGHEST, preferred_element_type=jnp.float32
    )


def half_rows(index, half):
    return pl.ds(pl.multiple_of(index * half, half), half)


def tiles_of(width):
    return COMPS // 8 * (width // LANES) + COMPS // 16


def put_cross_tiles(out, cross):
    across = cross.shape[1] // LANES
    for i in range(COMPS // 8):
        for j in range(across):
            out[i * across + j] = cross[i * 8 : i * 8 + 8, j * LANES : (j + 1) * LANES]


def put_gram_tiles(out, gram, first):
    for i in range(COMPS // 16):
        out[first + i] = jnp.concatenate(
            [gram[i * 16 : i * 16 + 8, :], gram[i * 16 + 8 : i * 16 + 16, :]], axis=1
        )


def take_tiles(tile, width):
    across = width // LANES
    cross = jnp.concatenate(
        [
            jnp.concatenate([tile(i * across + j) for j in range(across)], axis=1)
            for i in range(COMPS // 8)
        ],
        axis=0,
    )
    first = COMPS // 8 * across
    gram = []
    for i in range(COMPS // 16):
        pair = tile(first + i)
        gram += [pair[:, :COMPS], pair[:, COMPS:]]
    return cross, jnp.concatenate(gram, axis=0)


def pieces_of(width):
    return 2 * (width // LANES) + 1


def put_pieces(out, cross, gram):
    across = cross.shape[1] // LANES
    for share in range(8):
        for low in range(2):
            rows = slice(share * 8 + low * 4, share * 8 + low * 4 + 4)
            for j in range(across):
                out[share, 2 * j + low] = cross[rows, j * LANES : (j + 1) * LANES]
        upper, lower = gram[share * 8 : share * 8 + 4, :], gram[share * 8 + 4 : share * 8 + 8, :]
        out[share, 2 * across] = jnp.concatenate([upper, lower], axis=1)


def take_pieces(pieces, width):
    across = width // LANES
    cross, gram = [], []
    for share in range(8):
        tiles = [
            jnp.concatenate([pieces[share, 2 * j], pieces[share, 2 * j + 1]], axis=0)
            for j in range(across)
        ]
        cross.append(jnp.concatenate(tiles, axis=1))
        both = pieces[share, 2 * across]
        gram += [both[:, :COMPS], both[:, COMPS:]]
    return jnp.concatenate(cross, axis=0), jnp.concatenate(gram, axis=0)


def sweep(cross, gram, old, new, held, done=None):
    width = cross.shape[1]
    rows = lax.broadcasted_iota(jnp.int32, (COMPS, COMPS), 0)
    cols = lax.broadcasted_iota(jnp.int32, (COMPS, COMPS), 1)
    diag = jnp.sum(jnp.where(rows == cols, gram, 0.0), axis=1, keepdims=True)
    inverse = 1.0 / diag
    scaled = gram * inverse
    upper = jnp.where(cols > rows, scaled, 0.0)
    lower = jnp.where(cols < rows, scaled, 0.0)
    held[...] = cross * inverse - jnp.dot(
        upper, old, precision=lax.Precision.HIGHEST, preferred_element_type=jnp.float32
    )
    for block in range(0, COMPS, 8):
        own = held[block : block + 8, :]
        for index in range(7):
            row = jnp.maximum(own[index : index + 1, :], FLOOR)
            own = own - lower[block : block + 8, block + index : block + index + 1] * row
        own = jnp.maximum(own, FLOOR)
        new[block : block + 8, :] = own
        if done is not None:
            done(block // 8)
        for start in range(0, width, CHUNK):
            part = [own[i : i + 1, start : start + CHUNK] for i in range(8)]
            for later in range(block + 8, COMPS, 8):
                total = held[later : later + 8, start : start + CHUNK]
                for i in range(8):
                    total = total - lower[later : later + 8, block + i : block + i + 1] * part[i]
                held[later : later + 8, start : start + CHUNK] = total


def spec_cross(low, data):
    return lax.dot_general(low, data, NT, preferred_element_type=jnp.float32)


def spec_terms(core, spectra, data, out):
    half = data.shape[0] // 2
    cross = spec_cross(spectra.astype(jnp.bfloat16), data[half_rows(core, half), :])
    put_cross_tiles(out, cross)


def first_kernel(core, spec, data, send):
    spec_terms(1 - core[0], spec[...], data, send)
    put_gram_tiles(send, gram_of(spec[...]), send.shape[0] - COMPS // 16)


def spec_kernel(core, sums, old, data, new, send, held):
    cross, gram = take_pieces(sums, old.shape[1])
    sweep(cross, gram, old[...], new, held)
    first_kernel(core, new, data, send)


def keep_kernel(core, spec, data, send, keep):
    spec_terms(core[0], spec[...], data, keep)
    first = keep.shape[0] - COMPS // 16
    keep[first:] = send[first:]


def conc_sweep_kernel(core, parts, old, new, held):
    half = new.shape[1]
    cross, gram = take_tiles(
        lambda i: (parts[0, i] + parts[1, i]) + (parts[2, i] + parts[3, i]), half
    )
    if old.shape[1] == half:
        before = old[...]
    else:
        before = old[:, half_rows(core[0], half)]
    sweep(cross, gram, before, new, held)


def conc_terms(core, part, data):
    half = part.shape[1]
    cross = jnp.dot(
        part.astype(jnp.bfloat16), data[half_rows(core, half), :], preferred_element_type=jnp.float32
    )
    return cross, gram_of(part)


def own_terms_kernel(core, own, data, out):
    channels = data.shape[1]
    cross, gram = conc_terms(core[0], own[...], data)
    out[:, :channels] = cross
    out[:, channels : channels + COMPS] = gram
    out[:, channels + COMPS :] = jnp.zeros_like(out[:, channels + COMPS :])


def all_terms_kernel(core, other, data, own_terms, out):
    channels = data.shape[1]
    cross, gram = conc_terms(1 - core[0], other[...], data)
    put_pieces(
        out,
        own_terms[:, :channels] + cross,
        own_terms[:, channels : channels + COMPS] + gram,
    )


def last_kernel(core, sums, old, own, other, conc, spec, new, held, sems):
    half = own.shape[1]
    copies = [
        pltpu.make_async_copy(part, conc.at[:, half_rows(index, half)], sems.at[i])
        for i, (part, index) in enumerate(((own, core[0]), (other, 1 - core[0])))
    ]
    for copy in copies:
        copy.start()

    def done(block):
        rows = pl.ds(block * 8, 8)
        copies.append(pltpu.make_async_copy(new.at[rows, :], spec.at[rows, :], sems.at[2 + block]))
        copies[-1].start()

    cross, gram = take_pieces(sums, old.shape[1])
    sweep(cross, gram, old[...], new, held, done)
    for copy in copies:
        copy.wait()


def f32(*shape):
    return jax.ShapeDtypeStruct(shape, jnp.float32)


VMEM = pl.BlockSpec(memory_space=pltpu.VMEM)
SMEM = pl.BlockSpec(memory_space=pltpu.SMEM)
HBM = pl.BlockSpec(memory_space=pltpu.HBM)


def call(kernel, outs, specs, scratch, *args, space=VMEM):
    return pl.pallas_call(
        kernel,
        out_shape=outs,
        in_specs=specs,
        out_specs=jax.tree.map(lambda _: space, outs),
        scratch_shapes=scratch,
        compiler_params=pltpu.CompilerParams(vmem_limit_bytes=24 << 20),
        cost_estimate=pl.CostEstimate(
            flops=200_000_000, bytes_accessed=2_000_000, transcendentals=0
        ),
    )(*args)


def exchange(parts, axis, groups):
    return lax.all_to_all(parts, axis, 0, 0, axis_index_groups=groups)


def to_all(share, axis, groups):
    members = len(groups[0])
    return exchange(jnp.broadcast_to(share, (members,) + share.shape), axis, groups)


def swap(half):
    return lax.ppermute(half, "mass", SIBLING)


def sum_rows(terms):
    parts = exchange(terms, "rows", NEAR)
    parts = to_all(jnp.sum(parts, axis=0), "rows", FAR)
    return to_all(jnp.sum(parts, axis=0), "rows", NEAR)


def body(data, conc, spec):
    pixels, channels = data.shape
    half = pixels // 2
    core = lax.rem(lax.axis_index("mass"), 2).reshape(1)
    tiles, narrow = f32(tiles_of(half), 8, LANES), f32(COMPS, channels + LANES)
    pieces = f32(8, pieces_of(channels), 4, LANES)
    held = pltpu.VMEM((COMPS, half), jnp.float32)
    spec_held = pltpu.VMEM(spec.shape, jnp.float32)
    send = call(first_kernel, tiles, [SMEM, VMEM, VMEM], [], core, spec, data)
    own = conc
    for step in range(ITERS):
        arriving = swap(send)
        keep = call(keep_kernel, tiles, [SMEM, VMEM, VMEM, VMEM], [], core, spec, data, send)
        parts = to_all(keep + arriving, "mass", COLUMN)
        own = call(
            conc_sweep_kernel, f32(COMPS, half), [SMEM, VMEM, VMEM], [held], core, parts, own
        )
        other = swap(own)
        terms = call(own_terms_kernel, narrow, [SMEM, VMEM, VMEM], [], core, own, data)
        terms = call(
            all_terms_kernel, pieces, [SMEM, VMEM, VMEM, VMEM], [], core, other, data, terms
        )
        sums = sum_rows(terms)
        if step < ITERS - 1:
            spec, send = call(
                spec_kernel,
                (f32(*spec.shape), tiles),
                [SMEM, VMEM, VMEM, VMEM],
                [spec_held],
                core,
                sums,
                spec,
                data,
            )
        else:
            conc, spec = call(
                last_kernel,
                (f32(*conc.shape), f32(*spec.shape)),
                [SMEM, VMEM, VMEM, VMEM, VMEM],
                [spec_held, spec_held, pltpu.SemaphoreType.DMA((10,))],
                core,
                sums,
                spec,
                own,
                other,
                space=HBM,
            )
    return conc, spec


def solution(mesh):
    return jax.shard_map(
        body,
        mesh=mesh,
        in_specs=(P("rows", "mass"), P(None, "rows"), P(None, "mass")),
        out_specs=(P(None, "rows"), P(None, "mass")),
        check_vma=False,
    )
```

```python
import jax
import jax.numpy as jnp
from jax import lax
from jax.experimental import pallas as pl
from jax.experimental.pallas import tpu as pltpu
from jax.sharding import PartitionSpec as P

ITERS = 2
COMPS = 64
FLOOR = 1e-4
NT = (((1,), (1,)), ((), ()))
LANES = 128
CHUNK = 256


def holder(x, pair, low):
    return x * 16 + pair * 2 + (low ^ (pair >= 4))


FROM_MIDDLE = (2, 0, 1, 3)
PAIRS_FROM_MIDDLE = (4, 0, 5, 1, 6, 2, 7, 3)
NEAR = [[holder(x, pair, low) for low in range(2) for x in FROM_MIDDLE] for pair in range(8)]
FAR = [[holder(x, pair, low) for pair in PAIRS_FROM_MIDDLE] for x in range(4) for low in range(2)]
COLUMN = [[y * 2 + core for y in FROM_MIDDLE] for core in range(2)]
SIBLING = [(i, i ^ 1) for i in range(8)]


def gram_of(factor):
    return lax.dot_general(
        factor, factor, NT, precision=lax.Precision.HIGHEST, preferred_element_type=jnp.float32
    )


def half_rows(index, half):
    return pl.ds(pl.multiple_of(index * half, half), half)


def tiles_of(width):
    return COMPS // 8 * (width // LANES) + COMPS // 16


def put_cross_tiles(out, cross):
    across = cross.shape[1] // LANES
    for i in range(COMPS // 8):
        for j in range(across):
            out[i * across + j] = cross[i * 8 : i * 8 + 8, j * LANES : (j + 1) * LANES]


def put_gram_tiles(out, gram, first):
    for i in range(COMPS // 16):
        out[first + i] = jnp.concatenate(
            [gram[i * 16 : i * 16 + 8, :], gram[i * 16 + 8 : i * 16 + 16, :]], axis=1
        )


def take_tiles(tile, width):
    across = width // LANES
    cross = jnp.concatenate(
        [
            jnp.concatenate([tile(i * across + j) for j in range(across)], axis=1)
            for i in range(COMPS // 8)
        ],
        axis=0,
    )
    first = COMPS // 8 * across
    gram = []
    for i in range(COMPS // 16):
        pair = tile(first + i)
        gram += [pair[:, :COMPS], pair[:, COMPS:]]
    return cross, jnp.concatenate(gram, axis=0)


def pieces_of(width):
    return 2 * (width // LANES) + 1


def put_pieces(out, cross, gram):
    across = cross.shape[1] // LANES
    for share in range(8):
        for low in range(2):
            rows = slice(share * 8 + low * 4, share * 8 + low * 4 + 4)
            for j in range(across):
                out[share, 2 * j + low] = cross[rows, j * LANES : (j + 1) * LANES]
        upper, lower = gram[share * 8 : share * 8 + 4, :], gram[share * 8 + 4 : share * 8 + 8, :]
        out[share, 2 * across] = jnp.concatenate([upper, lower], axis=1)


def take_pieces(pieces, width):
    across = width // LANES
    cross, gram = [], []
    for share in range(8):
        tiles = [
            jnp.concatenate([pieces[share, 2 * j], pieces[share, 2 * j + 1]], axis=0)
            for j in range(across)
        ]
        cross.append(jnp.concatenate(tiles, axis=1))
        both = pieces[share, 2 * across]
        gram += [both[:, :COMPS], both[:, COMPS:]]
    return jnp.concatenate(cross, axis=0), jnp.concatenate(gram, axis=0)


def sweep(cross, gram, old, new, held, done=None):
    width = cross.shape[1]
    rows = lax.broadcasted_iota(jnp.int32, (COMPS, COMPS), 0)
    cols = lax.broadcasted_iota(jnp.int32, (COMPS, COMPS), 1)
    diag = jnp.sum(jnp.where(rows == cols, gram, 0.0), axis=1, keepdims=True)
    inverse = 1.0 / diag
    scaled = gram * inverse
    upper = jnp.where(cols > rows, scaled, 0.0)
    lower = jnp.where(cols < rows, scaled, 0.0)
    held[...] = cross * inverse - jnp.dot(
        upper, old, precision=lax.Precision.HIGHEST, preferred_element_type=jnp.float32
    )
    for block in range(0, COMPS, 8):
        own = held[block : block + 8, :]
        for index in range(7):
            row = jnp.maximum(own[index : index + 1, :], FLOOR)
            own = own - lower[block : block + 8, block + index : block + index + 1] * row
        own = jnp.maximum(own, FLOOR)
        new[block : block + 8, :] = own
        if done is not None:
            done(block // 8)
        for start in range(0, width, CHUNK):
            part = [own[i : i + 1, start : start + CHUNK] for i in range(8)]
            for later in range(block + 8, COMPS, 8):
                total = held[later : later + 8, start : start + CHUNK]
                for i in range(8):
                    total = total - lower[later : later + 8, block + i : block + i + 1] * part[i]
                held[later : later + 8, start : start + CHUNK] = total


def spec_cross(low, data):
    return lax.dot_general(low, data, NT, preferred_element_type=jnp.float32)


def spec_terms(core, spectra, data, out):
    half = data.shape[0] // 2
    cross = spec_cross(spectra.astype(jnp.bfloat16), data[half_rows(core, half), :])
    put_cross_tiles(out, cross)


def first_kernel(core, spec, data, send):
    spec_terms(1 - core[0], spec[...], data, send)
    put_gram_tiles(send, gram_of(spec[...]), send.shape[0] - COMPS // 16)


def spec_kernel(core, sums, old, data, new, send, held):
    cross, gram = take_pieces(sums, old.shape[1])
    sweep(cross, gram, old[...], new, held)
    first_kernel(core, new, data, send)


def keep_kernel(core, spec, data, send, keep):
    spec_terms(core[0], spec[...], data, keep)
    first = keep.shape[0] - COMPS // 16
    keep[first:] = send[first:]


def conc_sweep_kernel(core, parts, old, new, held):
    half = new.shape[1]
    cross, gram = take_tiles(
        lambda i: (parts[0, i] + parts[1, i]) + (parts[2, i] + parts[3, i]), half
    )
    if old.shape[1] == half:
        before = old[...]
    else:
        before = old[:, half_rows(core[0], half)]
    sweep(cross, gram, before, new, held)


def conc_terms(core, part, data):
    half = part.shape[1]
    cross = jnp.dot(
        part.astype(jnp.bfloat16), data[half_rows(core, half), :], preferred_element_type=jnp.float32
    )
    return cross, gram_of(part)


def own_terms_kernel(core, own, data, out):
    channels = data.shape[1]
    cross, gram = conc_terms(core[0], own[...], data)
    out[:, :channels] = cross
    out[:, channels : channels + COMPS] = gram
    out[:, channels + COMPS :] = jnp.zeros_like(out[:, channels + COMPS :])


def all_terms_kernel(core, other, data, own_terms, out):
    channels = data.shape[1]
    cross, gram = conc_terms(1 - core[0], other[...], data)
    put_pieces(
        out,
        own_terms[:, :channels] + cross,
        own_terms[:, channels : channels + COMPS] + gram,
    )


def last_kernel(core, sums, old, own, other, conc, spec, new, held, sems):
    half = own.shape[1]
    copies = [
        pltpu.make_async_copy(part, conc.at[:, half_rows(index, half)], sems.at[i])
        for i, (part, index) in enumerate(((own, core[0]), (other, 1 - core[0])))
    ]
    for copy in copies:
        copy.start()

    def done(block):
        rows = pl.ds(block * 8, 8)
        copies.append(pltpu.make_async_copy(new.at[rows, :], spec.at[rows, :], sems.at[2 + block]))
        copies[-1].start()

    cross, gram = take_pieces(sums, old.shape[1])
    sweep(cross, gram, old[...], new, held, done)
    for copy in copies:
        copy.wait()


def f32(*shape):
    return jax.ShapeDtypeStruct(shape, jnp.float32)


VMEM = pl.BlockSpec(memory_space=pltpu.VMEM)
SMEM = pl.BlockSpec(memory_space=pltpu.SMEM)
HBM = pl.BlockSpec(memory_space=pltpu.HBM)


def call(kernel, outs, specs, scratch, *args, space=VMEM):
    return pl.pallas_call(
        kernel,
        out_shape=outs,
        in_specs=specs,
        out_specs=jax.tree.map(lambda _: space, outs),
        scratch_shapes=scratch,
        compiler_params=pltpu.CompilerParams(vmem_limit_bytes=24 << 20),
        cost_estimate=pl.CostEstimate(
            flops=200_000_000, bytes_accessed=2_000_000, transcendentals=0
        ),
    )(*args)


def exchange(parts, axis, groups):
    return lax.all_to_all(parts, axis, 0, 0, axis_index_groups=groups)


def to_all(share, axis, groups):
    members = len(groups[0])
    return exchange(jnp.broadcast_to(share, (members,) + share.shape), axis, groups)


def swap(half):
    return lax.ppermute(half, "mass", SIBLING)


def sum_rows(terms):
    parts = exchange(terms, "rows", NEAR)
    parts = to_all(jnp.sum(parts, axis=0), "rows", FAR)
    return to_all(jnp.sum(parts, axis=0), "rows", NEAR)


def body(data, conc, spec):
    pixels, channels = data.shape
    half = pixels // 2
    core = lax.rem(lax.axis_index("mass"), 2).reshape(1)
    tiles, narrow = f32(tiles_of(half), 8, LANES), f32(COMPS, channels + LANES)
    pieces = f32(8, pieces_of(channels), 4, LANES)
    held = pltpu.VMEM((COMPS, half), jnp.float32)
    spec_held = pltpu.VMEM(spec.shape, jnp.float32)
    send = call(first_kernel, tiles, [SMEM, VMEM, VMEM], [], core, spec, data)
    own = conc
    for step in range(ITERS):
        arriving = swap(send)
        keep = call(keep_kernel, tiles, [SMEM, VMEM, VMEM, VMEM], [], core, spec, data, send)
        parts = to_all(keep + arriving, "mass", COLUMN)
        own = call(
            conc_sweep_kernel, f32(COMPS, half), [SMEM, VMEM, VMEM], [held], core, parts, own
        )
        other = swap(own)
        terms = call(own_terms_kernel, narrow, [SMEM, VMEM, VMEM], [], core, own, data)
        terms = call(
            all_terms_kernel, pieces, [SMEM, VMEM, VMEM, VMEM], [], core, other, data, terms
        )
        sums = sum_rows(terms)
        if step < ITERS - 1:
            spec, send = call(
                spec_kernel,
                (f32(*spec.shape), tiles),
                [SMEM, VMEM, VMEM, VMEM],
                [spec_held],
                core,
                sums,
                spec,
                data,
            )
        else:
            conc, spec = call(
                last_kernel,
                (f32(*conc.shape), f32(*spec.shape)),
                [SMEM, VMEM, VMEM, VMEM, VMEM],
                [spec_held, spec_held, pltpu.SemaphoreType.DMA((10,))],
                core,
                sums,
                spec,
                own,
                other,
                space=HBM,
            )
    return conc, spec


def solution(mesh):
    return jax.shard_map(
        body,
        mesh=mesh,
        in_specs=(P("rows", "mass"), P(None, "rows"), P(None, "mass")),
        out_specs=(P(None, "rows"), P(None, "mass")),
        check_vma=False,
    )
```

```python
import jax
import jax.numpy as jnp
from jax import lax
from jax.experimental import pallas as pl
from jax.experimental.pallas import tpu as pltpu
from jax.sharding import PartitionSpec as P

ITERS = 2
COMPS = 64
FLOOR = 1e-4
NT = (((1,), (1,)), ((), ()))
LANES = 128
CHUNK = 256


def holder(x, pair, low):
    return x * 16 + pair * 2 + (low ^ (pair >= 4))


FROM_MIDDLE = (2, 0, 1, 3)
PAIRS_FROM_MIDDLE = (4, 0, 5, 1, 6, 2, 7, 3)
NEAR = [[holder(x, pair, low) for low in range(2) for x in FROM_MIDDLE] for pair in range(8)]
FAR = [[holder(x, pair, low) for pair in PAIRS_FROM_MIDDLE] for x in range(4) for low in range(2)]
COLUMN = [[y * 2 for y in FROM_MIDDLE], [y * 2 + 1 for y in (2, 0, 3, 1)]]
SIBLING = [(i, i ^ 1) for i in range(8)]


def gram_of(factor):
    return lax.dot_general(
        factor, factor, NT, precision=lax.Precision.HIGHEST, preferred_element_type=jnp.float32
    )


def half_rows(index, half):
    return pl.ds(pl.multiple_of(index * half, half), half)


def tiles_of(width):
    return COMPS // 8 * (width // LANES) + COMPS // 16


def put_cross_tiles(out, cross):
    across = cross.shape[1] // LANES
    for i in range(COMPS // 8):
        for j in range(across):
            out[i * across + j] = cross[i * 8 : i * 8 + 8, j * LANES : (j + 1) * LANES]


def put_gram_tiles(out, gram, first):
    for i in range(COMPS // 16):
        out[first + i] = jnp.concatenate(
            [gram[i * 16 : i * 16 + 8, :], gram[i * 16 + 8 : i * 16 + 16, :]], axis=1
        )


def take_tiles(tile, width):
    across = width // LANES
    cross = jnp.concatenate(
        [
            jnp.concatenate([tile(i * across + j) for j in range(across)], axis=1)
            for i in range(COMPS // 8)
        ],
        axis=0,
    )
    first = COMPS // 8 * across
    gram = []
    for i in range(COMPS // 16):
        pair = tile(first + i)
        gram += [pair[:, :COMPS], pair[:, COMPS:]]
    return cross, jnp.concatenate(gram, axis=0)


def pieces_of(width):
    return 2 * (width // LANES) + 1


def put_pieces(out, cross, gram):
    across = cross.shape[1] // LANES
    for share in range(8):
        for low in range(2):
            rows = slice(share * 8 + low * 4, share * 8 + low * 4 + 4)
            for j in range(across):
                out[share, 2 * j + low] = cross[rows, j * LANES : (j + 1) * LANES]
        upper, lower = gram[share * 8 : share * 8 + 4, :], gram[share * 8 + 4 : share * 8 + 8, :]
        out[share, 2 * across] = jnp.concatenate([upper, lower], axis=1)


def take_pieces(pieces, width):
    across = width // LANES
    cross, gram = [], []
    for share in range(8):
        tiles = [
            jnp.concatenate([pieces[share, 2 * j], pieces[share, 2 * j + 1]], axis=0)
            for j in range(across)
        ]
        cross.append(jnp.concatenate(tiles, axis=1))
        both = pieces[share, 2 * across]
        gram += [both[:, :COMPS], both[:, COMPS:]]
    return jnp.concatenate(cross, axis=0), jnp.concatenate(gram, axis=0)


def sweep(cross, gram, old, new, held, done=None):
    width = cross.shape[1]
    rows = lax.broadcasted_iota(jnp.int32, (COMPS, COMPS), 0)
    cols = lax.broadcasted_iota(jnp.int32, (COMPS, COMPS), 1)
    diag = jnp.sum(jnp.where(rows == cols, gram, 0.0), axis=1, keepdims=True)
    inverse = 1.0 / diag
    scaled = gram * inverse
    upper = jnp.where(cols > rows, scaled, 0.0)
    lower = jnp.where(cols < rows, scaled, 0.0)
    held[...] = cross * inverse - jnp.dot(
        upper, old, precision=lax.Precision.HIGHEST, preferred_element_type=jnp.float32
    )
    for block in range(0, COMPS, 8):
        own = held[block : block + 8, :]
        for index in range(7):
            row = jnp.maximum(own[index : index + 1, :], FLOOR)
            own = own - lower[block : block + 8, block + index : block + index + 1] * row
        own = jnp.maximum(own, FLOOR)
        new[block : block + 8, :] = own
        if done is not None:
            done(block // 8)
        for start in range(0, width, CHUNK):
            part = [own[i : i + 1, start : start + CHUNK] for i in range(8)]
            for later in range(block + 8, COMPS, 8):
                total = held[later : later + 8, start : start + CHUNK]
                for i in range(8):
                    total = total - lower[later : later + 8, block + i : block + i + 1] * part[i]
                held[later : later + 8, start : start + CHUNK] = total


def spec_cross(low, data):
    return lax.dot_general(low, data, NT, preferred_element_type=jnp.float32)


def spec_terms(core, low, data, out):
    half = data.shape[0] // 2
    put_cross_tiles(out, spec_cross(low, data[half_rows(core, half), :]))


def gram_kernel(spec, gram, low):
    put_gram_tiles(gram, gram_of(spec[...]), 0)
    low[...] = spec[...].astype(jnp.bfloat16)


def first_kernel(core, low, gram, data, send):
    spec_terms(1 - core[0], low[...], data, send)
    send[send.shape[0] - COMPS // 16 :] = gram[...]


def spec_kernel(core, sums, old, data, new, send, held):
    cross, gram = take_pieces(sums, old.shape[1])
    sweep(cross, gram, old[...], new, held)
    spectra = new[...]
    spec_terms(1 - core[0], spectra.astype(jnp.bfloat16), data, send)
    put_gram_tiles(send, gram_of(spectra), send.shape[0] - COMPS // 16)


def keep_kernel(core, spec, data, send, keep):
    spec_terms(core[0], spec[...].astype(jnp.bfloat16), data, keep)
    first = keep.shape[0] - COMPS // 16
    keep[first:] = send[first:]


def conc_sweep_kernel(core, parts, old, new, held):
    half = new.shape[1]
    cross, gram = take_tiles(
        lambda i: (parts[0, i] + parts[1, i]) + (parts[2, i] + parts[3, i]), half
    )
    if old.shape[1] == half:
        before = old[...]
    else:
        before = old[:, half_rows(core[0], half)]
    sweep(cross, gram, before, new, held)


def conc_terms(core, part, data):
    half = part.shape[1]
    cross = jnp.dot(
        part.astype(jnp.bfloat16), data[half_rows(core, half), :], preferred_element_type=jnp.float32
    )
    return cross, gram_of(part)


def own_terms_kernel(core, own, data, out):
    channels = data.shape[1]
    cross, gram = conc_terms(core[0], own[...], data)
    out[:, :channels] = cross
    out[:, channels : channels + COMPS] = gram
    out[:, channels + COMPS :] = jnp.zeros_like(out[:, channels + COMPS :])


def all_terms_kernel(core, other, data, own_terms, out):
    channels = data.shape[1]
    cross, gram = conc_terms(1 - core[0], other[...], data)
    put_pieces(
        out,
        own_terms[:, :channels] + cross,
        own_terms[:, channels : channels + COMPS] + gram,
    )


def last_kernel(core, sums, old, own, other, conc, spec, new, held, sems):
    half = own.shape[1]
    copies = [
        pltpu.make_async_copy(part, conc.at[:, half_rows(index, half)], sems.at[i])
        for i, (part, index) in enumerate(((own, core[0]), (other, 1 - core[0])))
    ]
    for copy in copies:
        copy.start()

    def done(block):
        rows = pl.ds(block * 8, 8)
        copies.append(pltpu.make_async_copy(new.at[rows, :], spec.at[rows, :], sems.at[2 + block]))
        copies[-1].start()

    cross, gram = take_pieces(sums, old.shape[1])
    sweep(cross, gram, old[...], new, held, done)
    for copy in copies:
        copy.wait()


def f32(*shape):
    return jax.ShapeDtypeStruct(shape, jnp.float32)


VMEM = pl.BlockSpec(memory_space=pltpu.VMEM)
SMEM = pl.BlockSpec(memory_space=pltpu.SMEM)
HBM = pl.BlockSpec(memory_space=pltpu.HBM)


def call(kernel, outs, specs, scratch, *args, space=VMEM, flops=200_000_000):
    return pl.pallas_call(
        kernel,
        out_shape=outs,
        in_specs=specs,
        out_specs=jax.tree.map(lambda _: space, outs),
        scratch_shapes=scratch,
        compiler_params=pltpu.CompilerParams(vmem_limit_bytes=24 << 20),
        cost_estimate=pl.CostEstimate(
            flops=flops, bytes_accessed=2_000_000, transcendentals=0
        ),
    )(*args)


def exchange(parts, axis, groups):
    return lax.all_to_all(parts, axis, 0, 0, axis_index_groups=groups)


def to_all(share, axis, groups):
    members = len(groups[0])
    return exchange(jnp.broadcast_to(share, (members,) + share.shape), axis, groups)


def swap(half):
    return lax.ppermute(half, "mass", SIBLING)


def sum_rows(terms):
    parts = exchange(terms, "rows", NEAR)
    parts = to_all(jnp.sum(parts, axis=0), "rows", FAR)
    return to_all(jnp.sum(parts, axis=0), "rows", NEAR)


def body(data, conc, spec):
    pixels, channels = data.shape
    half = pixels // 2
    core = lax.rem(lax.axis_index("mass"), 2).reshape(1)
    tiles, narrow = f32(tiles_of(half), 8, LANES), f32(COMPS, channels + LANES)
    pieces = f32(8, pieces_of(channels), 4, LANES)
    held = pltpu.VMEM((COMPS, half), jnp.float32)
    spec_held = pltpu.VMEM(spec.shape, jnp.float32)
    gram, low = call(
        gram_kernel,
        (f32(COMPS // 16, 8, LANES), jax.ShapeDtypeStruct(spec.shape, jnp.bfloat16)),
        [VMEM],
        [],
        spec,
        flops=4_000_000_000,
    )
    send = call(first_kernel, tiles, [SMEM, VMEM, VMEM, VMEM], [], core, low, gram, data)
    own = conc
    for step in range(ITERS):
        arriving = swap(send)
        keep = call(keep_kernel, tiles, [SMEM, VMEM, VMEM, VMEM], [], core, spec, data, send)
        parts = to_all(keep + arriving, "mass", COLUMN)
        own = call(
            conc_sweep_kernel, f32(COMPS, half), [SMEM, VMEM, VMEM], [held], core, parts, own
        )
        other = swap(own)
        terms = call(own_terms_kernel, narrow, [SMEM, VMEM, VMEM], [], core, own, data)
        terms = call(
            all_terms_kernel, pieces, [SMEM, VMEM, VMEM, VMEM], [], core, other, data, terms
        )
        sums = sum_rows(terms)
        if step < ITERS - 1:
            spec, send = call(
                spec_kernel,
                (f32(*spec.shape), tiles),
                [SMEM, VMEM, VMEM, VMEM],
                [spec_held],
                core,
                sums,
                spec,
                data,
            )
        else:
            conc, spec = call(
                last_kernel,
                (f32(*conc.shape), f32(*spec.shape)),
                [SMEM, VMEM, VMEM, VMEM, VMEM],
                [spec_held, spec_held, pltpu.SemaphoreType.DMA((10,))],
                core,
                sums,
                spec,
                own,
                other,
                space=HBM,
            )
    return conc, spec


def solution(mesh):
    return jax.shard_map(
        body,
        mesh=mesh,
        in_specs=(P("rows", "mass"), P(None, "rows"), P(None, "mass")),
        out_specs=(P(None, "rows"), P(None, "mass")),
        check_vma=False,
    )
```

```python
import jax
import jax.numpy as jnp
from jax import lax
from jax.experimental import pallas as pl
from jax.experimental.pallas import tpu as pltpu
from jax.sharding import PartitionSpec as P

ITERS = 2
COMPS = 64
FLOOR = 1e-4
NT = (((1,), (1,)), ((), ()))
LANES = 128
CHUNK = 256


def holder(x, pair, low):
    return x * 16 + pair * 2 + (low ^ (pair >= 4))


FROM_MIDDLE = (2, 0, 1, 3)
PAIRS_FROM_MIDDLE = (4, 0, 1, 7, 2, 6, 3, 5)
NEAR = [[holder(x, pair, low) for low in range(2) for x in FROM_MIDDLE] for pair in range(8)]
FAR = [[holder(x, pair, low) for pair in PAIRS_FROM_MIDDLE] for x in range(4) for low in range(2)]
COLUMN = [[y * 2 for y in FROM_MIDDLE], [y * 2 + 1 for y in (2, 0, 3, 1)]]
SIBLING = [(i, i ^ 1) for i in range(8)]


def gram_of(factor):
    return lax.dot_general(
        factor, factor, NT, precision=lax.Precision.HIGHEST, preferred_element_type=jnp.float32
    )


def half_rows(index, half):
    return pl.ds(pl.multiple_of(index * half, half), half)


def tiles_of(width):
    return COMPS // 8 * (width // LANES) + COMPS // 16


def put_cross_tiles(out, cross):
    across = cross.shape[1] // LANES
    for i in range(COMPS // 8):
        for j in range(across):
            out[i * across + j] = cross[i * 8 : i * 8 + 8, j * LANES : (j + 1) * LANES]


def put_gram_tiles(out, gram, first):
    for i in range(COMPS // 16):
        out[first + i] = jnp.concatenate(
            [gram[i * 16 : i * 16 + 8, :], gram[i * 16 + 8 : i * 16 + 16, :]], axis=1
        )


def take_tiles(tile, width):
    across = width // LANES
    cross = jnp.concatenate(
        [
            jnp.concatenate([tile(i * across + j) for j in range(across)], axis=1)
            for i in range(COMPS // 8)
        ],
        axis=0,
    )
    first = COMPS // 8 * across
    gram = []
    for i in range(COMPS // 16):
        pair = tile(first + i)
        gram += [pair[:, :COMPS], pair[:, COMPS:]]
    return cross, jnp.concatenate(gram, axis=0)


def pieces_of(width):
    return 2 * (width // LANES) + 1


def put_pieces(out, cross, gram):
    across = cross.shape[1] // LANES
    for share in range(8):
        for low in range(2):
            rows = slice(share * 8 + low * 4, share * 8 + low * 4 + 4)
            for j in range(across):
                out[share, 2 * j + low] = cross[rows, j * LANES : (j + 1) * LANES]
        upper, lower = gram[share * 8 : share * 8 + 4, :], gram[share * 8 + 4 : share * 8 + 8, :]
        out[share, 2 * across] = jnp.concatenate([upper, lower], axis=1)


def take_pieces(pieces, width):
    across = width // LANES
    cross, gram = [], []
    for share in range(8):
        tiles = [
            jnp.concatenate([pieces[share, 2 * j], pieces[share, 2 * j + 1]], axis=0)
            for j in range(across)
        ]
        cross.append(jnp.concatenate(tiles, axis=1))
        both = pieces[share, 2 * across]
        gram += [both[:, :COMPS], both[:, COMPS:]]
    return jnp.concatenate(cross, axis=0), jnp.concatenate(gram, axis=0)


def sweep(cross, gram, old, new, held, done=None):
    width = cross.shape[1]
    rows = lax.broadcasted_iota(jnp.int32, (COMPS, COMPS), 0)
    cols = lax.broadcasted_iota(jnp.int32, (COMPS, COMPS), 1)
    diag = jnp.sum(jnp.where(rows == cols, gram, 0.0), axis=1, keepdims=True)
    inverse = 1.0 / diag
    scaled = gram * inverse
    upper = jnp.where(cols > rows, scaled, 0.0)
    lower = jnp.where(cols < rows, scaled, 0.0)
    held[...] = cross * inverse - jnp.dot(
        upper, old, precision=lax.Precision.HIGHEST, preferred_element_type=jnp.float32
    )
    for block in range(0, COMPS, 8):
        own = held[block : block + 8, :]
        for index in range(7):
            row = jnp.maximum(own[index : index + 1, :], FLOOR)
            own = own - lower[block : block + 8, block + index : block + index + 1] * row
        own = jnp.maximum(own, FLOOR)
        new[block : block + 8, :] = own
        if done is not None:
            done(block // 8)
        for start in range(0, width, CHUNK):
            part = [own[i : i + 1, start : start + CHUNK] for i in range(8)]
            for later in range(block + 8, COMPS, 8):
                total = held[later : later + 8, start : start + CHUNK]
                for i in range(8):
                    total = total - lower[later : later + 8, block + i : block + i + 1] * part[i]
                held[later : later + 8, start : start + CHUNK] = total


def spec_cross(low, data):
    return lax.dot_general(low, data, NT, preferred_element_type=jnp.float32)


def spec_terms(core, low, data, out):
    half = data.shape[0] // 2
    put_cross_tiles(out, spec_cross(low, data[half_rows(core, half), :]))


def gram_kernel(spec, gram, low):
    put_gram_tiles(gram, gram_of(spec[...]), 0)
    low[...] = spec[...].astype(jnp.bfloat16)


def first_kernel(core, low, gram, data, send):
    spec_terms(1 - core[0], low[...], data, send)
    send[send.shape[0] - COMPS // 16 :] = gram[...]


def spec_kernel(core, sums, old, data, new, send, held):
    cross, gram = take_pieces(sums, old.shape[1])
    sweep(cross, gram, old[...], new, held)
    spectra = new[...]
    spec_terms(1 - core[0], spectra.astype(jnp.bfloat16), data, send)
    put_gram_tiles(send, gram_of(spectra), send.shape[0] - COMPS // 16)


def keep_kernel(core, spec, data, send, keep):
    spec_terms(core[0], spec[...].astype(jnp.bfloat16), data, keep)
    first = keep.shape[0] - COMPS // 16
    keep[first:] = send[first:]


def conc_sweep_kernel(core, parts, old, new, held):
    half = new.shape[1]
    cross, gram = take_tiles(
        lambda i: (parts[0, i] + parts[1, i]) + (parts[2, i] + parts[3, i]), half
    )
    if old.shape[1] == half:
        before = old[...]
    else:
        before = old[:, half_rows(core[0], half)]
    sweep(cross, gram, before, new, held)


def conc_terms(core, part, data):
    half = part.shape[1]
    cross = jnp.dot(
        part.astype(jnp.bfloat16), data[half_rows(core, half), :], preferred_element_type=jnp.float32
    )
    return cross, gram_of(part)


def own_terms_kernel(core, own, data, out):
    channels = data.shape[1]
    cross, gram = conc_terms(core[0], own[...], data)
    out[:, :channels] = cross
    out[:, channels : channels + COMPS] = gram
    out[:, channels + COMPS :] = jnp.zeros_like(out[:, channels + COMPS :])


def all_terms_kernel(core, other, data, own_terms, out):
    channels = data.shape[1]
    cross, gram = conc_terms(1 - core[0], other[...], data)
    put_pieces(
        out,
        own_terms[:, :channels] + cross,
        own_terms[:, channels : channels + COMPS] + gram,
    )


def last_kernel(core, sums, old, own, other, conc, spec, new, held, sems):
    half = own.shape[1]
    copies = [
        pltpu.make_async_copy(part, conc.at[:, half_rows(index, half)], sems.at[i])
        for i, (part, index) in enumerate(((own, core[0]), (other, 1 - core[0])))
    ]
    for copy in copies:
        copy.start()

    def done(block):
        rows = pl.ds(block * 8, 8)
        copies.append(pltpu.make_async_copy(new.at[rows, :], spec.at[rows, :], sems.at[2 + block]))
        copies[-1].start()

    cross, gram = take_pieces(sums, old.shape[1])
    sweep(cross, gram, old[...], new, held, done)
    for copy in copies:
        copy.wait()


def f32(*shape):
    return jax.ShapeDtypeStruct(shape, jnp.float32)


VMEM = pl.BlockSpec(memory_space=pltpu.VMEM)
SMEM = pl.BlockSpec(memory_space=pltpu.SMEM)
HBM = pl.BlockSpec(memory_space=pltpu.HBM)


def call(kernel, outs, specs, scratch, *args, space=VMEM, flops=200_000_000):
    return pl.pallas_call(
        kernel,
        out_shape=outs,
        in_specs=specs,
        out_specs=jax.tree.map(lambda _: space, outs),
        scratch_shapes=scratch,
        compiler_params=pltpu.CompilerParams(vmem_limit_bytes=24 << 20),
        cost_estimate=pl.CostEstimate(
            flops=flops, bytes_accessed=2_000_000, transcendentals=0
        ),
    )(*args)


def exchange(parts, axis, groups):
    return lax.all_to_all(parts, axis, 0, 0, axis_index_groups=groups)


def to_all(share, axis, groups):
    members = len(groups[0])
    return exchange(jnp.broadcast_to(share, (members,) + share.shape), axis, groups)


def swap(half):
    return lax.ppermute(half, "mass", SIBLING)


def sum_rows(terms):
    parts = exchange(terms, "rows", NEAR)
    parts = to_all(jnp.sum(parts, axis=0), "rows", FAR)
    return to_all(jnp.sum(parts, axis=0), "rows", NEAR)


def body(data, conc, spec):
    pixels, channels = data.shape
    half = pixels // 2
    core = lax.rem(lax.axis_index("mass"), 2).reshape(1)
    tiles, narrow = f32(tiles_of(half), 8, LANES), f32(COMPS, channels + LANES)
    pieces = f32(8, pieces_of(channels), 4, LANES)
    held = pltpu.VMEM((COMPS, half), jnp.float32)
    spec_held = pltpu.VMEM(spec.shape, jnp.float32)
    gram, low = call(
        gram_kernel,
        (f32(COMPS // 16, 8, LANES), jax.ShapeDtypeStruct(spec.shape, jnp.bfloat16)),
        [VMEM],
        [],
        spec,
        flops=4_000_000_000,
    )
    send = call(first_kernel, tiles, [SMEM, VMEM, VMEM, VMEM], [], core, low, gram, data)
    own = conc
    for step in range(ITERS):
        arriving = swap(send)
        keep = call(keep_kernel, tiles, [SMEM, VMEM, VMEM, VMEM], [], core, spec, data, send)
        parts = to_all(keep + arriving, "mass", COLUMN)
        own = call(
            conc_sweep_kernel, f32(COMPS, half), [SMEM, VMEM, VMEM], [held], core, parts, own
        )
        other = swap(own)
        terms = call(own_terms_kernel, narrow, [SMEM, VMEM, VMEM], [], core, own, data)
        terms = call(
            all_terms_kernel, pieces, [SMEM, VMEM, VMEM, VMEM], [], core, other, data, terms
        )
        sums = sum_rows(terms)
        if step < ITERS - 1:
            spec, send = call(
                spec_kernel,
                (f32(*spec.shape), tiles),
                [SMEM, VMEM, VMEM, VMEM],
                [spec_held],
                core,
                sums,
                spec,
                data,
            )
        else:
            conc, spec = call(
                last_kernel,
                (f32(*conc.shape), f32(*spec.shape)),
                [SMEM, VMEM, VMEM, VMEM, VMEM],
                [spec_held, spec_held, pltpu.SemaphoreType.DMA((10,))],
                core,
                sums,
                spec,
                own,
                other,
                space=HBM,
            )
    return conc, spec


def solution(mesh):
    return jax.shard_map(
        body,
        mesh=mesh,
        in_specs=(P("rows", "mass"), P(None, "rows"), P(None, "mass")),
        out_specs=(P(None, "rows"), P(None, "mass")),
        check_vma=False,
    )
```
